512 devices in a mesh: member: 16 (over z_lo, y), space: 32 (over z_hi, x, core).
Axes of the slice: x: 4, y: 8, z: 8 (z_hi: 4, z_lo: 2; z = z_hi * 2 + z_lo), core: 2. Of those that a mesh axis runs over, the one named last changes fastest.
Arguments:
- ensemble: float32 [64, 512, 2048], P('member', 'space'), may hold values from -6 to 6
- spreading_number: float32 [512, 2048], P('space'), may hold values from 0.05 to 0.2
- zonal_transport_ratio: float32 [512, 2048], P('space'), may hold values from -0.2 to 0.2
- meridional_transport_ratio: float32 [512, 2048], P('space'), may hold values from -0.2 to 0.2
- ocean_mask: int32 [512, 2048], P('space'), may hold values 0 or 1
- obs_loc: int32 [65536], replicated, may hold values from 0 to 1048575, as said below
- obs_value: float32 [65536], replicated, may hold values from -6 to 6
- obs_sigma: float32 [65536], replicated, may hold values from 0.3 to 1
- tile_obs: int32 [512, 16, 256], P('space'), may hold values from 0 to 65535, as said below
Outputs:
- analysis: float32 [64, 512, 2048], P('member', 'space')
The draws below stay inside these ranges and needn't reach their ends.
Inputs may be any that keep to these rules, and one draw needn't show every extreme that they name: `obs_loc`: observation j lies in grid rows (j // 2048) * 16 to (j // 2048 + 1) * 16 - 1. `tile_obs`: the observations named for a tile in grid row r have indices from (r // 16 - 1) * 2048 to (r // 16 + 2) * 2048 - 1; repeats may occur.
All inputs are finite; a program needn't handle non-finite values. No bound on the sum of `ocean_mask` on one device may be relied on, other than what follows from the above.
Results may differ from the reference program's by a relative error of at most 0.0003.
Values sent between devices are 32-bit elements; how exact they have to be, the bound alone decides.
A program may use at most 64 MiB of HBM per device.

```python
import math
import jax
import jax.numpy as jnp
from jax import lax

MEMBERS = 64
CY = 16
NX = 2048
NY = 512
TILE_COLS = 128
OBS_DEV = 2048
OBS_ALL = 65536
OBS_TILE = 256
LOC_RADIUS = 96
NS_ITERS = 6


def draw_obs_loc(key, part):
    subkeys = jax.random.split(key, 2)
    obs_index = jnp.arange(OBS_ALL, dtype=jnp.int32)
    owner_tile = obs_index // OBS_DEV
    local_index = obs_index % OBS_DEV
    jitter = max(NX // OBS_DEV, 1)
    grid_row = owner_tile * CY + jax.random.randint(subkeys[0], (OBS_ALL,), 0, CY)
    grid_col = local_index * NX // OBS_DEV + jax.random.randint(subkeys[1], (OBS_ALL,), 0, jitter)
    return (grid_row * NX + grid_col).astype(jnp.int32)


def draw_tile_obs(key, part):
    subkeys = jax.random.split(key, 2)
    out_shape = (NY, NX // TILE_COLS, OBS_TILE)
    grid_row = jnp.arange(NY, dtype=jnp.int32).reshape(NY, 1, 1)
    tile_col = jnp.arange(NX // TILE_COLS, dtype=jnp.int32).reshape(1, NX // TILE_COLS, 1)
    home_tile = grid_row // CY
    near_tile = jnp.clip(home_tile + jax.random.randint(subkeys[0], out_shape, -1, 2), 0, NY // CY - 1)
    col_span = TILE_COLS * OBS_DEV // NX
    offset = jax.random.randint(subkeys[1], out_shape, -col_span, 2 * col_span)
    local_index = (tile_col * col_span + offset) % OBS_DEV
    return (near_tile * OBS_DEV + local_index).astype(jnp.int32)


def plant(array, stream_key, least, largest):
    place = [jax.random.randint(jax.random.fold_in(stream_key, axis), (), 0, length) for axis, length in enumerate(array.shape)]
    longest = array.shape.index(max(array.shape))
    next_to = place[:longest] + [(place[longest] + 1) % array.shape[longest]] + place[longest + 1:]
    return array.at[tuple(place)].set(least).at[tuple(next_to)].set(largest)


def level_of(key, shape, cuts, least, high):
    gain, own = 1.0, jax.random.fold_in(key, 6)
    for dim, parts in cuts:
        draws = jnp.exp(jax.random.uniform(jax.random.fold_in(own, dim), (parts,), jnp.float32, least / len(cuts), high / len(cuts)))
        gain = gain * jnp.repeat(draws, shape[dim] // parts).reshape([-1 if axis == dim else 1 for axis in range(len(shape))])
    return gain


def noise(stream_key, shape, width, reach, cuts=(), held_as=jnp.bfloat16):
    level = level_of(stream_key, shape, cuts, -0.22, 0.18) if cuts else 1.0
    values = jax.random.normal(stream_key, shape, jnp.float32) * width * level
    return jnp.minimum(jnp.maximum(values, -reach), reach).astype(held_as)


def setup_inputs(seed: int = 0) -> dict:
    arg_keys = jax.random.split(jax.random.key(seed), 10)
    return {
        "ensemble": noise(arg_keys[0], (MEMBERS, NY, NX), 1.0, 6.0, ((0, 16), (1, 32)), jnp.float32),
        "spreading_number": jnp.clip(0.05 + 0.15 * jax.random.uniform(arg_keys[1], (NY, NX), jnp.float32) ** level_of(arg_keys[1], (NY, NX), ((0, 32),), -0.2, 0.2), 0.05, 0.2),
        "zonal_transport_ratio": jnp.clip(jax.random.uniform(arg_keys[2], (NY, NX), jnp.float32, -0.2, 0.2) * level_of(arg_keys[2], (NY, NX), ((0, 32),), -0.4, 0.0), -0.2, 0.2),
        "meridional_transport_ratio": jnp.clip(jax.random.uniform(arg_keys[3], (NY, NX), jnp.float32, -0.2, 0.2) * level_of(arg_keys[3], (NY, NX), ((0, 32),), -0.4, 0.0), -0.2, 0.2),
        "ocean_mask": plant((jax.random.randint(arg_keys[4], (NY, NX), 0, 10) < 7).astype(jnp.int32), jax.random.fold_in(arg_keys[4], 1), 0, 1),
        "obs_loc": draw_obs_loc(jax.random.fold_in(arg_keys[9], 71), 0),
        "obs_value": noise(arg_keys[6], (OBS_ALL,), 1.0, 6.0, (), jnp.float32),
        "obs_sigma": jnp.clip(jnp.exp(jax.random.uniform(arg_keys[7], (OBS_ALL,), jnp.float32, math.log(0.3), math.log(1.0))), 0.3, 1.0),
        "tile_obs": draw_tile_obs(jax.random.fold_in(arg_keys[9], 71), 0),
    }


highest = lax.Precision.HIGHEST

def propagate_prior_state(haloed_state_grid, spreading_number, zonal_transport_ratio, meridional_transport_ratio, liquid_cell_flags):
    centre = haloed_state_grid[:, 1:-1, :]
    northern = haloed_state_grid[:, 2:, :]
    southern = haloed_state_grid[:, :-2, :]
    eastern = jnp.roll(centre, -1, axis=2)
    western = jnp.roll(centre, 1, axis=2)
    laplace = northern + southern + eastern + western - 4.0 * centre
    advect = zonal_transport_ratio * (eastern - western) * 0.5 + meridional_transport_ratio * (northern - southern) * 0.5
    return liquid_cell_flags * (centre + spreading_number * laplace - advect)

def analyze(ensemble_block, anomalies, means, window_picks, global_picks, obs_loc, obs_value, obs_sigma, row_first, col_first, grid_cols):
    members, block_rows, block_cols = ensemble_block.shape
    tile_cols = block_cols // TILE_COLS
    tile_count = block_rows * tile_cols
    window_flat = window_picks.reshape(tile_count, -1)
    global_flat = global_picks.reshape(tile_count, -1)
    chosen = jnp.take(anomalies, window_flat, axis=1)
    chosen_mean = jnp.take(means, window_flat)
    location = jnp.take(obs_loc, global_flat)
    obs_row = location // grid_cols
    obs_col = location % grid_cols
    zero_grid = jnp.zeros((block_rows, tile_cols), jnp.int32)
    tile_row = (row_first + jnp.arange(block_rows, dtype=jnp.int32)[:, None] + zero_grid).reshape(tile_count, 1)
    tile_start = (col_first + TILE_COLS * jnp.arange(tile_cols, dtype=jnp.int32)[None, :] + zero_grid).reshape(tile_count, 1)
    row_gap = (obs_row - tile_row).astype(jnp.float32)
    col_twice = 2 * obs_col - 2 * tile_start - (TILE_COLS - 1)
    col_twice = (col_twice + grid_cols) % (2 * grid_cols) - grid_cols
    col_gap = 0.5 * col_twice.astype(jnp.float32)
    distance = row_gap * row_gap + col_gap * col_gap
    tapering = jnp.exp(-distance / (2.0 * LOC_RADIUS * LOC_RADIUS))
    sigma_sel = jnp.take(obs_sigma, global_flat)
    obs_weight = tapering / (sigma_sel * sigma_sel)
    innovation = jnp.take(obs_value, global_flat) - chosen_mean
    weighted = chosen * obs_weight[None]
    gram_matrix = jnp.einsum('knl,jnl->nkj', weighted, chosen, precision=highest)
    identity = jnp.eye(members, dtype=jnp.float32)
    system = gram_matrix + (members - 1.0) * identity
    frob_norm = jnp.sqrt(lax.optimization_barrier(jnp.sum(system * system, axis=(1, 2))))
    iterate = system / frob_norm[:, None, None]
    inverse_root = jnp.broadcast_to(identity, system.shape)
    for sweep_index in range(NS_ITERS):
        factor = 1.5 * identity - 0.5 * jnp.einsum('nij,njk->nik', inverse_root, iterate, precision=highest)
        iterate = jnp.einsum('nij,njk->nik', iterate, factor, precision=highest)
        inverse_root = jnp.einsum('nij,njk->nik', factor, inverse_root, precision=highest)
    forcing = jnp.einsum('knl,nl->nk', chosen, obs_weight * innovation, precision=highest)
    half_step = jnp.einsum('nkj,nj->nk', inverse_root, forcing, precision=highest)
    mean_weight = jnp.einsum('nkj,nj->nk', inverse_root, half_step, precision=highest) / frob_norm[:, None]
    transform = jnp.sqrt(members - 1.0) * inverse_root / jnp.sqrt(frob_norm)[:, None, None] + mean_weight[:, :, None]
    tile_cells = ensemble_block.reshape(members, tile_count, TILE_COLS)
    centre_mean = lax.optimization_barrier(jnp.mean(tile_cells, axis=0))
    spread = tile_cells - centre_mean
    analysis = centre_mean + jnp.einsum('jnt,njk->knt', spread, transform, precision=highest)
    return analysis.reshape(members, block_rows, block_cols)

def reference(ensemble, spreading_number, zonal_transport_ratio, meridional_transport_ratio, ocean_mask, obs_loc, obs_value, obs_sigma, tile_obs):
    liquid_cell_flags = ocean_mask.astype(jnp.float32)
    level_state_grid = liquid_cell_flags * ensemble
    for prior_step_tally in range(2):
        haloed_state_grid = jnp.pad(level_state_grid, ((0, 0), (1, 1), (0, 0)))
        level_state_grid = propagate_prior_state(haloed_state_grid, spreading_number, zonal_transport_ratio, meridional_transport_ratio, liquid_cell_flags)
    members = level_state_grid.shape[0]
    observed = jnp.take(level_state_grid.reshape(members, NY * NX), obs_loc, axis=1)
    obs_mean = lax.optimization_barrier(jnp.mean(observed, axis=0))
    obs_anom = observed - obs_mean
    band_count = NY // CY
    blocks = level_state_grid.reshape(members, band_count, CY, NX).transpose(1, 0, 2, 3)
    all_picks = tile_obs.reshape(band_count, CY, NX // TILE_COLS, OBS_TILE)

    def one_block(operands):
        ensemble_block, chosen_picks, block_index = operands
        return analyze(ensemble_block, obs_anom, obs_mean, chosen_picks, chosen_picks, obs_loc, obs_value, obs_sigma, block_index * CY, 0, NX)
    result = lax.map(one_block, (blocks, all_picks, jnp.arange(band_count, dtype=jnp.int32)))
    return result.transpose(1, 0, 2, 3).reshape(members, NY, NX)
```

```python
import functools

import jax
import jax.numpy as jnp
from jax import lax
from jax.experimental import pallas as pl
from jax.experimental.pallas import tpu as pltpu
from jax.sharding import PartitionSpec as P

LOC_RADIUS = 96
MESH = pl.DeviceIdType.MESH
f32 = jnp.float32
bf16 = jnp.bfloat16
i32 = jnp.int32
MEM = 16
NYD = 8
SPACE = 32
KM = 4
ROWS = 16
COLS = 2048
OBS = 2048


def split(x):
    hi = x.astype(bf16)
    return hi, (x - hi.astype(f32)).astype(bf16)


def mm(a, b):
    return jnp.dot(a, b, preferred_element_type=f32)


def mm3(a, b):
    ah, al = split(a)
    bh, bl = split(b)
    return mm(ah, bh) + (mm(al, bh) + mm(ah, bl))


def forecast(ens, spr, zon, mer, mask, hu_lo, hc_lo, hu_hi, hc_hi, field, first, last):
    s, z, m = spr[...], zon[...] * 0.5, mer[...] * 0.5
    sea = mask[...].astype(f32)

    def step(centre, north, south, s, z, m, sea):
        east = pltpu.roll(centre, COLS - 1, 1)
        west = pltpu.roll(centre, 1, 1)
        lap = north + south + east + west - 4.0 * centre
        adv = z * (east - west) + m * (north - south)
        return sea * (centre + s * lap - adv)

    lo = jnp.where(first, 0.0, hu_lo[...])
    hi = jnp.where(last, 0.0, hu_hi[...])
    south2, south1 = lo[0:KM], lo[KM:]
    north1, north2 = hi[0:KM], hi[KM:]
    own_first = jnp.concatenate([sea[0:1] * ens[k, 0:1] for k in range(KM)], axis=0)
    own_last = jnp.concatenate([sea[ROWS - 1 :] * ens[k, ROWS - 1 :] for k in range(KM)], axis=0)

    def coef(ref, edge):
        c = ref[...]
        return c[0:1], c[1:2] * 0.5, c[2:3] * 0.5, jnp.where(edge, 0.0, c[3:4])

    below = step(south1, own_first, south2, *coef(hc_lo, first))
    above = step(north1, north2, own_last, *coef(hc_hi, last))
    for k in range(KM):
        u = sea * ens[k]
        north = jnp.concatenate([u[1:], north1[k : k + 1]], axis=0)
        south = jnp.concatenate([south1[k : k + 1], u[: ROWS - 1]], axis=0)
        u = step(u, north, south, s, z, m, sea)
        north = jnp.concatenate([u[1:], above[k : k + 1]], axis=0)
        south = jnp.concatenate([below[k : k + 1], u[: ROWS - 1]], axis=0)
        field[k] = step(u, north, south, s, z, m, sea)


def observe(field, loc, hx):
    sub = lax.broadcasted_iota(i32, (8, 128), 0)

    def body(g, _):
        at = loc[1, pl.ds(g, 1), :]
        row = jnp.broadcast_to((at >> 11) & (ROWS - 1), (8, 128))
        blk = jnp.broadcast_to((at >> 7) & 15, (8, 128))
        lane = jnp.broadcast_to(at & 127, (8, 128))
        acc = [jnp.zeros((8, 128), f32) for _ in range(2 * KM)]
        for b in range(16):
            hit = blk == b
            for k in range(KM):
                for h in range(2):
                    v = field[k, 8 * h : 8 * h + 8, 128 * b : 128 * b + 128]
                    got = jnp.take_along_axis(v, lane, axis=1, mode="promise_in_bounds")
                    acc[2 * k + h] = jnp.where(hit, got, acc[2 * k + h])
        for k in range(KM):
            mine = jnp.where(row == sub, acc[2 * k], 0.0) + jnp.where(
                row == sub + 8, acc[2 * k + 1], 0.0
            )
            hx[g & 7, pl.ds((g >> 3) * KM + k, 1), :] = jnp.sum(mine, axis=0, keepdims=True)
        return 0

    lax.fori_loop(0, 16, body, 0)


def weigh(lo, hi, picks, loc, val, sig, rinv, vals, row0, mid2):
    sub = lax.broadcasted_iota(i32, (8, 128), 0)

    def body(p, _):
        ix = picks[pl.ds(p, 1), :]
        blk = jnp.broadcast_to(ix >> 7, (8, 128))
        lane = jnp.broadcast_to(ix & 127, (8, 128))
        acc = [jnp.zeros((8, 128), i32), jnp.zeros((8, 128), f32), jnp.zeros((8, 128), f32)]
        for v in range(6):
            hit = (blk - 8 * v) == sub
            for q, ref in enumerate((loc, val, sig)):
                got = jnp.take_along_axis(
                    ref[v // 2, 8 * (v % 2) : 8 * (v % 2) + 8, :],
                    lane,
                    axis=1,
                    mode="promise_in_bounds",
                )
                acc[q] = jnp.where(hit, got, acc[q])
        at, value, sigma = [jnp.sum(a, axis=0, keepdims=True) for a in acc]
        row_gap = ((at >> 11) - (row0 + (p >> 1))).astype(f32)
        twice = 2 * (at & (COLS - 1)) - mid2
        twice = ((twice + COLS) & (2 * COLS - 1)) - COLS
        col_gap = 0.5 * twice.astype(f32)
        distance = row_gap * row_gap + col_gap * col_gap
        taper = jnp.exp(-distance / (2.0 * LOC_RADIUS * LOC_RADIUS))
        rinv[pl.ds(p, 1), :] = taper / (sigma * sigma)
        vals[pl.ds(p, 1), :] = value
        return 0

    lax.fori_loop(lo, hi, body, 0)


def tabulate(band, win, table):
    def body(cb, _):
        vs = [win[band, m, cb] for m in range(MEM)]
        for half in range(2):
            x = jnp.concatenate([v[KM * half : KM * half + KM] for v in vs], axis=0)
            mean = jnp.sum(x, axis=0, keepdims=True) * (1.0 / 64)
            full = jnp.concatenate([x - mean, jnp.broadcast_to(mean, (64, 128))], axis=0)
            at = band * OBS + half * 1024 + cb * 128
            table[pl.ds(pl.multiple_of(at, 128), 128), :] = full.T
        return 0

    lax.fori_loop(0, 8, body, 0)


def fetch(t, idx, table, chosen, unroll=32):
    def body(j, _):
        rows = []
        for u in range(unroll):
            i = j * unroll + u
            rows.append(table[pl.ds(idx[2 * t + (i >> 7), i & 127], 1), :])
        for u in range(unroll):
            chosen[pl.ds(j * unroll + u, 1), :] = rows[u]
        return 0

    lax.fori_loop(0, 256 // unroll, body, 0)


def gram(t, chosen, rinv, vals, start, force, scale):
    a = chosen[...]
    at = a.T
    r = jnp.concatenate([rinv[pl.ds(2 * t, 1), :], rinv[pl.ds(2 * t + 1, 1), :]], axis=1)
    v = jnp.concatenate([vals[pl.ds(2 * t, 1), :], vals[pl.ds(2 * t + 1, 1), :]], axis=1)
    w = jnp.concatenate(
        [at[0:64] * r, jnp.broadcast_to(r * (v - at[64:65]), (8, 256))], axis=0
    )
    g = mm3(w, a)
    ii = lax.broadcasted_iota(i32, (64, 128), 0)
    jj = lax.broadcasted_iota(i32, (64, 128), 1)
    system = jnp.where(jj < 64, g[0:64], 0.0) + jnp.where(ii == jj, 63.0, 0.0)
    square = jnp.sum(jnp.sum(system * system, axis=0, keepdims=True), axis=1, keepdims=True)
    inv = lax.rsqrt(square)
    start[t] = system * inv
    force[pl.ds(t, 1), :] = g[64:65]
    scale[pl.ds(t, 1), :] = jnp.broadcast_to(inv, (1, 128))


def pack(start, t):
    def pair(a, b):
        lane = lax.broadcasted_iota(i32, a.shape, 1)
        return jnp.where(lane < 64, a, pltpu.roll(b, 64, 1))

    return jnp.concatenate(
        [pair(start[t], start[t + 1]), pair(start[t + 2], start[t + 3])], axis=1
    )


def diagonal(x):
    quarter = lax.broadcasted_iota(i32, x.shape, 1) >> 6
    return jnp.concatenate(
        [jnp.where(quarter == i, x, jnp.zeros_like(x)) for i in range(4)], axis=0
    ).astype(bf16)


def newton(xs):
    ii = lax.broadcasted_iota(i32, (64, 256), 0)
    jj = lax.broadcasted_iota(i32, (64, 256), 1) & 63
    eye = jnp.where(ii == jj, 1.5, 0.0).astype(f32)
    zs = None

    def dot(left, right):
        h, l = split(left)
        return mm(h, right[0]) + (mm(l, right[0]) + mm(h, right[1]))

    for it in range(6):
        fs = [eye - 0.5 * x for x in xs]
        blocks = []
        for f in fs:
            h, l = split(f)
            blocks.append((diagonal(h.astype(f32)), diagonal(l.astype(f32))))
        if it == 0:
            ps = [dot(x, b) for x, b in zip(xs, blocks)]
            zs = fs
            xs = [dot(p, b) for p, b in zip(ps, blocks)]
        elif it < 5:
            both = [
                dot(jnp.concatenate([x, z], axis=0), b) for x, z, b in zip(xs, zs, blocks)
            ]
            zs = [q[64:] for q in both]
            xs = [dot(q[:64], b) for q, b in zip(both, blocks)]
        else:
            zs = [dot(z, b) for z, b in zip(zs, blocks)]
    return zs


def transform_pair(t, z, force, scale, cells, out):
    lane = lax.broadcasted_iota(i32, (64, 128), 1)
    lane1 = lane[0:1]
    g = jnp.where(lane1 < 64, force[pl.ds(t, 1), :], pltpu.roll(force[pl.ds(t + 1, 1), :], 64, 1))
    inv = jnp.where(lane1 < 64, scale[pl.ds(t, 1), :], scale[pl.ds(t + 1, 1), :])
    q = z * g
    h0 = jnp.sum(jnp.where(lane < 64, q, 0.0), axis=1, keepdims=True)
    h1 = jnp.sum(jnp.where(lane < 64, 0.0, q), axis=1, keepdims=True)
    wbar = jnp.sum(z * jnp.where(lane < 64, h0, h1), axis=0, keepdims=True) * inv
    weights = jnp.sqrt(63.0 * inv) * z + wbar
    xs, means = [], []
    for i in range(2):
        x = cells[pl.ds(t + i, 64, stride=ROWS), :]
        mean = jnp.sum(x, axis=0, keepdims=True) * (1.0 / 64)
        xs.append(x - mean)
        means.append(mean)
    none = jnp.zeros((64, 128), f32)
    block = jnp.concatenate(
        [jnp.concatenate([xs[0], none], axis=1), jnp.concatenate([none, xs[1]], axis=1)], axis=0
    )
    moved = mm3(weights, block)
    for i in range(2):
        out[pl.ds(t + i, 64, stride=ROWS), :] = means[i] + moved[:, 128 * i : 128 * i + 128]


PARTS = 2


def kernel(
    ens_h, spr_h, zon_h, mer_h, mask_h, loc_h, val_h, sig_h, tile_h, out,
    ens, spr, zon, mer, mask, loc, val, sig, tile, picks, idx,
    send_u, send_c, hu_lo, hc_lo, hu_hi, hc_hi, field, hx, win, rinv, vals, table, chosen,
    start, force, scale, cells, done,
    load_sem, obs_sem, halo_send, halo_recv, y_send, y_recv, z_send, z_recv,
    lo_send, lo_recv, hi_send, hi_recv, c_send, c_recv, a_send, a_recv, local_sem,
):
    me = lax.axis_index("member")
    sp = lax.axis_index("space")
    zz, yy = me // NYD, me % NYD
    below, above = (sp + SPACE - 1) % SPACE, (sp + 1) % SPACE
    other = me ^ NYD

    loads = [
        pltpu.make_async_copy(a, b, load_sem.at[i])
        for i, (a, b) in enumerate(
            [(ens_h, ens), (mask_h, mask), (spr_h, spr), (zon_h, zon), (mer_h, mer), (tile_h, tile)]
        )
    ]
    for j in range(3):
        band = jnp.clip(sp - 1 + j, 0, SPACE - 1)
        for i, (a, b) in enumerate([(loc_h, loc), (val_h, val), (sig_h, sig)]):
            loads.append(pltpu.make_async_copy(a.at[band], b.at[j], obs_sem.at[3 * j + i]))
    for copy in loads:
        copy.start()

    barrier = pltpu.get_barrier_semaphore()
    for i in range(1, MEM):
        pl.semaphore_signal(barrier, inc=1, device_id=((me + i) % MEM, sp), device_id_type=MESH)
    for to in (below, above):
        pl.semaphore_signal(barrier, inc=1, device_id=(me, to), device_id_type=MESH)
    for copy in loads[:5]:
        copy.wait()

    for side, (r1, r2, edge) in enumerate([(0, 1, 0), (ROWS - 2, ROWS - 1, ROWS - 1)]):
        for j, r in enumerate((r1, r2)):
            sea = mask[r : r + 1, :].astype(f32)
            for k in range(KM):
                send_u[side, j * KM + k : j * KM + k + 1, :] = sea * ens[k, r : r + 1, :]
        for q, ref in enumerate((spr, zon, mer)):
            send_c[side, q : q + 1, :] = ref[edge : edge + 1, :]
        send_c[side, 3:4, :] = mask[edge : edge + 1, :].astype(f32)
    pl.semaphore_wait(barrier, MEM + 1)

    def remote(src, dst, send, recv, to):
        return pltpu.make_async_remote_copy(
            src_ref=src, dst_ref=dst, send_sem=send, recv_sem=recv, device_id=to, device_id_type=MESH
        )

    halos = [
        remote(send_u.at[0], hu_hi, halo_send.at[0], halo_recv.at[0], (me, below)),
        remote(send_c.at[0], hc_hi, halo_send.at[1], halo_recv.at[1], (me, below)),
        remote(send_u.at[1], hu_lo, halo_send.at[2], halo_recv.at[2], (me, above)),
        remote(send_c.at[1], hc_lo, halo_send.at[3], halo_recv.at[3], (me, above)),
    ]
    for copy in halos:
        copy.start()
    for copy in loads[5:]:
        copy.wait()
    first_obs = (sp - 1) * OBS
    for r in range(ROWS):
        row = jnp.clip(tile[r, pl.ds(me, 1), :] - first_obs, 0, 3 * OBS - 1)
        picks[2 * r : 2 * r + 1, :] = row[:, 0:128]
        picks[2 * r + 1 : 2 * r + 2, :] = row[:, 128:256]
    to_scalar = pltpu.make_async_copy(picks, idx, local_sem.at[0])
    to_scalar.start()
    for copy in halos:
        copy.wait()

    forecast(ens, spr, zon, mer, mask, hu_lo, hc_lo, hu_hi, hc_hi, field, sp == 0, sp == SPACE - 1)
    observe(field, loc, hx)

    def to_lo(src, slot, i):
        return remote(src, win.at[2, slot], lo_send.at[i], lo_recv.at[i], (me, below))

    def to_hi(src, slot, i):
        return remote(src, win.at[0, slot], hi_send.at[i], hi_recv.at[i], (me, above))

    def to_z(src, slot, i):
        return remote(src, win.at[1, slot], z_send.at[i], z_recv.at[i], (other, sp))

    keep = pltpu.make_async_copy(hx, win.at[1, me], local_sem.at[1])
    keep.start()
    steps = (1, 7, 2, 6, 3, 5, 4)
    ys = [
        remote(hx, win.at[1, me], y_send.at[i], y_recv.at[i], (zz * NYD + (yy + d) % NYD, sp))
        for i, d in enumerate(steps)
    ]
    zs, los, his = [to_z(hx, me, 0)], [to_lo(hx, me, 0)], [to_hi(hx, me, 0)]
    for copy in ys + zs + los + his:
        copy.start()
    row0, mid2 = sp * ROWS, 2 * 128 * me + 127

    def some(i):
        weigh(2 * i, 2 * i + 2, picks, loc, val, sig, rinv, vals, row0, mid2)

    for i, d in enumerate(steps):
        some(i)
        ys[i].wait_recv()
        slot = zz * NYD + (yy + NYD - d) % NYD
        src = win.at[1, slot]
        zs.append(to_z(src, slot, i + 1))
        los.append(to_lo(src, slot, i + 1))
        his.append(to_hi(src, slot, i + 1))
        for copy in (zs[-1], los[-1], his[-1]):
            copy.start()
    for i, d in enumerate((0,) + steps):
        some(7 + i)
        zs[i].wait_recv()
        slot = (1 - zz) * NYD + (yy + NYD - d) % NYD
        src = win.at[1, slot]
        los.append(to_lo(src, slot, i + 8))
        his.append(to_hi(src, slot, i + 8))
        for copy in (los[-1], his[-1]):
            copy.start()
    some(15)

    cs = []
    for i in range(1, MEM):
        to = (me + i) % MEM
        cs.append(
            remote(
                field.at[:, :, pl.ds(pl.multiple_of(128 * to, 128), 128)],
                cells.at[pl.ds(KM * me, KM)],
                c_send.at[i],
                c_recv.at[i],
                (to, sp),
            )
        )
        cs[-1].start()
    own = pltpu.make_async_copy(
        field.at[:, :, pl.ds(pl.multiple_of(128 * me, 128), 128)],
        cells.at[pl.ds(KM * me, KM)],
        local_sem.at[2],
    )
    own.start()

    keep.wait()
    tabulate(1, win, table)
    for copy in his:
        copy.wait_recv()
    tabulate(0, win, table)
    for copy in los:
        copy.wait_recv()
    tabulate(2, win, table)
    to_scalar.wait()

    def tile_body(t, _):
        fetch(t, idx, table, chosen)
        gram(t, chosen, rinv, vals, start, force, scale)
        return 0

    lax.fori_loop(0, ROWS, tile_body, 0)
    own.wait()
    for copy in cs:
        copy.wait_recv()

    flat_cells = cells.reshape(64 * ROWS, 128)
    flat_done = done.reshape(64 * ROWS, 128)
    outs = []
    each = ROWS // PARTS
    for part in range(PARTS):
        t0 = part * each
        zq = newton([pack(start, t0 + 4 * i) for i in range(each // 4)])
        for i in range(each // 4):
            for j in range(2):
                transform_pair(
                    t0 + 4 * i + 2 * j,
                    zq[i][:, 128 * j : 128 * j + 128],
                    force,
                    scale,
                    flat_cells,
                    flat_done,
                )
        rows = pl.ds(t0, each)
        mine = pl.ds(pl.multiple_of(128 * me, 128), 128)
        for i in range(1, MEM):
            to = (me + i) % MEM
            outs.append(
                remote(
                    done.at[pl.ds(KM * to, KM), rows, :],
                    out.at[:, rows, mine],
                    a_send.at[part * MEM + i],
                    a_recv.at[part * MEM + i],
                    (to, sp),
                )
            )
            outs[-1].start()
        last = pltpu.make_async_copy(
            done.at[pl.ds(KM * me, KM), rows, :], out.at[:, rows, mine], local_sem.at[3 + part]
        )
        last.start()
        outs.append(last)
    for copy in ys + zs + los + his + cs:
        copy.wait_send()
    for copy in outs:
        copy.wait()


def on_device(ensemble, spreading, zonal, meridional, ocean, obs_loc, obs_value, obs_sigma, tile_obs):
    vm, dma = pltpu.VMEM, pltpu.SemaphoreType.DMA
    return pl.pallas_call(
        kernel,
        out_shape=jax.ShapeDtypeStruct((KM, ROWS, COLS), f32),
        in_specs=[pl.BlockSpec(memory_space=pl.ANY)] * 9,
        out_specs=pl.BlockSpec(memory_space=pltpu.VMEM),
        scratch_shapes=[
            vm((KM, ROWS, COLS), f32), vm((ROWS, COLS), f32), vm((ROWS, COLS), f32),
            vm((ROWS, COLS), f32), vm((ROWS, COLS), i32),
            vm((3, 16, 128), i32), vm((3, 16, 128), f32), vm((3, 16, 128), f32),
            vm((ROWS, 16, 256), i32), vm((32, 128), i32), pltpu.SMEM((32, 128), i32),
            vm((2, 2 * KM, COLS), f32), vm((2, 4, COLS), f32),
            vm((2 * KM, COLS), f32), vm((4, COLS), f32), vm((2 * KM, COLS), f32), vm((4, COLS), f32),
            vm((KM, ROWS, COLS), f32), vm((8, 8, 128), f32), vm((3, MEM, 8, 8, 128), f32),
            vm((32, 128), f32), vm((32, 128), f32), vm((3 * OBS, 128), f32), vm((256, 128), f32),
            vm((16, 64, 128), f32), vm((16, 128), f32), vm((16, 128), f32),
            vm((64, ROWS, 128), f32), vm((64, ROWS, 128), f32),
            dma((6,)), dma((9,)), dma((4,)), dma((4,)), dma((7,)), dma((7,)), dma((8,)), dma((8,)),
            dma((16,)), dma((16,)), dma((16,)), dma((16,)), dma((MEM,)), dma((MEM,)),
            dma((PARTS * MEM,)), dma((PARTS * MEM,)), dma((3 + PARTS,)),
        ],
        compiler_params=pltpu.CompilerParams(
            collective_id=0, has_side_effects=True, vmem_limit_bytes=40 << 20
        ),
    )(
        ensemble, spreading, zonal, meridional, ocean,
        obs_loc.reshape(SPACE, 16, 128), obs_value.reshape(SPACE, 16, 128),
        obs_sigma.reshape(SPACE, 16, 128), tile_obs,
    )


def solution(mesh):
    in_specs = (
        P("member", "space", None),
        P("space", None),
        P("space", None),
        P("space", None),
        P("space", None),
        P(),
        P(),
        P(),
        P("space", None, None),
    )
    return jax.shard_map(
        on_device,
        mesh=mesh,
        in_specs=in_specs,
        out_specs=P("member", "space", None),
        check_vma=False,
    )
```
